512 devices in a mesh: row: 32 (over z, y_lo), col: 16 (over y_hi, x, core).
Axes of the slice: x: 4, y: 8 (y_hi: 2, y_lo: 4; y = y_hi * 4 + y_lo), z: 8, core: 2. Of those that a mesh axis runs over, the one named last changes fastest.
Arguments:
- pair: bfloat16 [448, 448, 128], P('row', 'col'), may hold values from -6 to 6
- out_norm_gain: float32 [128], replicated, may hold values from 0.1 to 1.9
- out_norm_bias: float32 [128], replicated, may hold values from -3 to 3
- out_weight_in: bfloat16 [128, 640], replicated, may hold values from -0.5 to 0.5
- out_mix_gain: float32 [128], replicated, may hold values from 0.1 to 1.9
- out_mix_bias: float32 [128], replicated, may hold values from -3 to 3
- out_weight_out: bfloat16 [128, 128], replicated, may hold values from -0.5 to 0.5
- in_norm_gain: float32 [128], replicated, may hold values from 0.1 to 1.9
- in_norm_bias: float32 [128], replicated, may hold values from -3 to 3
- in_weight_in: bfloat16 [128, 640], replicated, may hold values from -0.5 to 0.5
- in_mix_gain: float32 [128], replicated, may hold values from 0.1 to 1.9
- in_mix_bias: float32 [128], replicated, may hold values from -3 to 3
- in_weight_out: bfloat16 [128, 128], replicated, may hold values from -0.5 to 0.5
Outputs:
- updated: bfloat16 [448, 448, 128], P('row', 'col')
The draws below stay inside these ranges and needn't reach their ends.
All inputs are finite; a program needn't handle non-finite values.
Results may differ from the reference program's by a relative error of at most 0.013.
Values may be sent and summed in bfloat16 or wider, within the bound.
No kernel may reach another device: no remote copies, remote signals or barrier semaphores. Data moves between devices by JAX's collectives and lax.ppermute only.
A program may use at most 64 MiB of HBM per device.

```python
import jax
import jax.numpy as jnp
from jax import lax

C = 128
CH = 128
N = 448


def block_levels(rng, dims, split, low, top_value):
    level, own = 1.0, jax.random.fold_in(rng, 6)
    for position, blocks in split:
        draws = jnp.exp(jax.random.uniform(jax.random.fold_in(own, position), (blocks,), jnp.float32, low / len(split), top_value / len(split)))
        level = level * jnp.repeat(draws, dims[position] // blocks).reshape([-1 if axis == position else 1 for axis in range(len(dims))])
    return level


def normal_values(stream_key, dims, scale, most, cuts=(), kind=jnp.bfloat16):
    result = jax.random.normal(stream_key, dims, jnp.float32) * scale
    if len(cuts) > 0:
        result = block_levels(stream_key, dims, cuts, -0.22, 0.18) * result
    return jnp.clip(result, min=-most, max=most).astype(kind)


def setup_inputs(seed: int = 0) -> dict:
    seeds = jax.random.split(jax.random.key(seed), 14)
    pair = normal_values(seeds[0], (N, N, C), 1.0, 6.0, ((0, 32), (1, 16)))
    out_norm_gain = jnp.clip(1.0 + 0.18 * jax.random.normal(seeds[1], (C,), jnp.float32), 0.1, 1.9)
    out_norm_bias = normal_values(seeds[2], (C,), 0.5, 3.0, (), jnp.float32)
    out_weight_in = normal_values(seeds[3], (C, 4 * CH + C), C ** -0.5, 0.5)
    out_mix_gain = jnp.clip(1.0 + 0.18 * jax.random.normal(seeds[4], (CH,), jnp.float32), 0.1, 1.9)
    out_mix_bias = normal_values(seeds[5], (CH,), 0.5, 3.0, (), jnp.float32)
    out_weight_out = normal_values(seeds[6], (CH, C), CH ** -0.5, 0.5)
    in_norm_gain = jnp.clip(1.0 + 0.18 * jax.random.normal(seeds[7], (C,), jnp.float32), 0.1, 1.9)
    in_norm_bias = normal_values(seeds[8], (C,), 0.5, 3.0, (), jnp.float32)
    in_weight_in = normal_values(seeds[9], (C, 4 * CH + C), C ** -0.5, 0.5)
    in_mix_gain = jnp.clip(1.0 + 0.18 * jax.random.normal(seeds[10], (CH,), jnp.float32), 0.1, 1.9)
    in_mix_bias = normal_values(seeds[11], (CH,), 0.5, 3.0, (), jnp.float32)
    in_weight_out = normal_values(seeds[12], (CH, C), CH ** -0.5, 0.5)
    return {"pair": pair, "out_norm_gain": out_norm_gain, "out_norm_bias": out_norm_bias, "out_weight_in": out_weight_in, "out_mix_gain": out_mix_gain, "out_mix_bias": out_mix_bias, "out_weight_out": out_weight_out, "in_norm_gain": in_norm_gain, "in_norm_bias": in_norm_bias, "in_weight_in": in_weight_in, "in_mix_gain": in_mix_gain, "in_mix_bias": in_mix_bias, "in_weight_out": in_weight_out}


EPSILON = 1e-05

def layer_norm(values, gain, bias):
    center = values - lax.optimization_barrier(jnp.mean(values, axis=-1, keepdims=True))
    spread = lax.optimization_barrier(jnp.mean(center * center, axis=-1, keepdims=True))
    return center * lax.rsqrt(spread + EPSILON) * gain + bias

def project(pair, gain, bias, weight_in):
    normed = layer_norm(pair.astype(jnp.float32), gain, bias).astype(jnp.bfloat16)
    projected = jnp.dot(normed, weight_in, preferred_element_type=jnp.float32)
    left_operand = (jax.nn.sigmoid(projected[..., :CH]) * projected[..., CH:2 * CH]).astype(jnp.bfloat16)
    right_operand = (jax.nn.sigmoid(projected[..., 2 * CH:3 * CH]) * projected[..., 3 * CH:4 * CH]).astype(jnp.bfloat16)
    gating = jax.nn.sigmoid(projected[..., 4 * CH:])
    return (left_operand, right_operand, gating)

def finish(pair, mixed, gating, gain, bias, weight_out):
    normed = layer_norm(mixed, gain, bias).astype(jnp.bfloat16)
    update = gating * jnp.dot(normed, weight_out, preferred_element_type=jnp.float32)
    return (pair.astype(jnp.float32) + update).astype(jnp.bfloat16)

def reference(pair, out_norm_gain, out_norm_bias, out_weight_in, out_mix_gain, out_mix_bias, out_weight_out, in_norm_gain, in_norm_bias, in_weight_in, in_mix_gain, in_mix_bias, in_weight_out):
    left_operand, right_operand, gating = project(pair, out_norm_gain, out_norm_bias, out_weight_in)
    mixed = jnp.einsum('ikc,jkc->ijc', left_operand.astype(jnp.float32), right_operand.astype(jnp.float32), precision=lax.Precision.HIGHEST)
    first = finish(pair, mixed, gating, out_mix_gain, out_mix_bias, out_weight_out)
    left_operand, right_operand, gating = project(first, in_norm_gain, in_norm_bias, in_weight_in)
    mixed = jnp.einsum('kic,kjc->ijc', left_operand.astype(jnp.float32), right_operand.astype(jnp.float32), precision=lax.Precision.HIGHEST)
    return finish(first, mixed, gating, in_mix_gain, in_mix_bias, in_weight_out)
```

```python
import jax
import jax.numpy as jnp
from jax import lax
from jax.sharding import Mesh, PartitionSpec as P

CH = 128
EPSILON = 1e-05

ROW = ("z", "ylo")
COL = ("yhi", "x", "core")
OUT_GROUP = ("z", "yhi", "x", "core")
IN_GROUP = ("z", "ylo", "yhi", "core")


def layer_norm(values, gain, bias):
    center = values - jnp.mean(values, axis=-1, keepdims=True)
    spread = jnp.mean(center * center, axis=-1, keepdims=True)
    return center * lax.rsqrt(spread + EPSILON) * gain + bias


def project_all(pair, gain, bias, weight_in):
    normed = layer_norm(pair.astype(jnp.float32), gain, bias).astype(jnp.bfloat16)
    projected = jnp.einsum("ijc,cd->ijd", normed, weight_in, preferred_element_type=jnp.float32)
    left = jax.nn.sigmoid(projected[..., :CH]) * projected[..., CH : 2 * CH]
    right = jax.nn.sigmoid(projected[..., 2 * CH : 3 * CH]) * projected[..., 3 * CH : 4 * CH]
    gating = jax.nn.sigmoid(projected[..., 4 * CH :])
    both = jnp.stack([left, right]).astype(jnp.bfloat16)
    return both.transpose(3, 0, 1, 2), gating


def finish(pair, mixed, gating, gain, bias, weight_out):
    normed = layer_norm(mixed, gain, bias).astype(jnp.bfloat16)
    update = gating * jnp.einsum(
        "ijc,cd->ijd", normed, weight_out, preferred_element_type=jnp.float32
    )
    return (pair.astype(jnp.float32) + update).astype(jnp.bfloat16)


def exchange(values, group):
    return lax.all_to_all(values, group, 0, 0, tiled=True)


def shards(pair, og, ob, owi, omg, omb, owo, ig, ib, iwi, img, imb, iwo):
    rows, cols, _ = pair.shape
    both, gating = project_all(pair, og, ob, owi)
    both = exchange(both, OUT_GROUP).reshape(8, 16, 2, rows, cols)
    both = both.transpose(2, 0, 3, 1, 4).reshape(2, 8, rows, 16 * cols)
    left = both[0].reshape(8 * rows, 16 * cols)
    right = lax.all_gather(both[1], "ylo", axis=1).reshape(32 * rows, 16 * cols)
    mixed = jnp.einsum("ik,jk->ij", left, right, preferred_element_type=jnp.float32)
    mixed = mixed.astype(jnp.bfloat16).reshape(8, rows, 16, cols).transpose(0, 2, 1, 3)
    mixed = exchange(mixed.reshape(128, rows, cols), OUT_GROUP)
    mixed = mixed.transpose(1, 2, 0).astype(jnp.float32)
    first = finish(pair, mixed, gating, omg, omb, owo)

    both, gating = project_all(first, ig, ib, iwi)
    both = exchange(both, IN_GROUP).reshape(32, 2, 2, 2, rows, cols)
    both = both.transpose(3, 0, 4, 1, 2, 5).reshape(2, 32 * rows, 2, 2, cols)
    left = lax.all_gather(both[0], "x", axis=2).reshape(32 * rows, 16 * cols)
    right = both[1].reshape(32 * rows, 4 * cols)
    mixed = jnp.einsum("ki,kj->ij", left, right, preferred_element_type=jnp.float32)
    mixed = mixed.astype(jnp.bfloat16).reshape(32, rows, 4, cols).transpose(0, 2, 1, 3)
    mixed = exchange(mixed.reshape(128, rows, cols), IN_GROUP)
    mixed = mixed.transpose(1, 2, 0).astype(jnp.float32)
    return finish(first, mixed, gating, img, imb, iwo)


def solution(mesh):
    fine = Mesh(mesh.devices.reshape(8, 4, 2, 4, 2), ("z", "ylo", "yhi", "x", "core"))
    return jax.shard_map(
        shards,
        mesh=fine,
        in_specs=(P(ROW, COL, None),) + (P(),) * 12,
        out_specs=P(ROW, COL, None),
        check_vma=False,
    )
```

```python
import jax
import jax.numpy as jnp
from jax import lax
from jax.sharding import Mesh, PartitionSpec as P

CH = 128
EPSILON = 1e-05

AXES = ("zh", "zl", "ylo", "yhi", "xh", "xl", "core")
ROW, COL = AXES[:3], AXES[3:]
OUT_GROUP = ("zh", "ylo", "yhi", "xh", "xl")
IN_GROUP = ("zh", "zl", "ylo", "yhi", "xl")


def layer_norm(values, gain, bias):
    center = values - jnp.mean(values, axis=-1, keepdims=True)
    spread = jnp.mean(center * center, axis=-1, keepdims=True)
    return center * lax.rsqrt(spread + EPSILON) * gain + bias


def project_all(pair, gain, bias, weight_in):
    normed = layer_norm(pair.astype(jnp.float32), gain, bias).astype(jnp.bfloat16)
    projected = jnp.einsum("ijc,cd->ijd", normed, weight_in, preferred_element_type=jnp.float32)
    left = jax.nn.sigmoid(projected[..., :CH]) * projected[..., CH : 2 * CH]
    right = jax.nn.sigmoid(projected[..., 2 * CH : 3 * CH]) * projected[..., 3 * CH : 4 * CH]
    gating = jax.nn.sigmoid(projected[..., 4 * CH :])
    both = jnp.stack([left, right]).astype(jnp.bfloat16)
    return both.transpose(3, 0, 1, 2), gating


def finish(pair, mixed, gating, gain, bias, weight_out):
    normed = layer_norm(mixed, gain, bias).astype(jnp.bfloat16)
    update = gating * jnp.einsum(
        "ijc,cd->ijd", normed, weight_out, preferred_element_type=jnp.float32
    )
    return (pair.astype(jnp.float32) + update).astype(jnp.bfloat16)


def exchange(values, group):
    return lax.all_to_all(values, group, 0, 0, tiled=True)


def shards(pair, og, ob, owi, omg, omb, owo, ig, ib, iwi, img, imb, iwo):
    rows, cols, _ = pair.shape
    both, gating = project_all(pair, og, ob, owi)
    both = exchange(both, OUT_GROUP).reshape(16, 8, 2, rows, cols)
    both = both.transpose(2, 0, 3, 1, 4).reshape(2, 16 * rows, 8 * cols)
    left = lax.all_gather(both[0], "core", axis=0)
    right = lax.all_gather(both[1], ("zl", "core"), axis=0)
    right = right.reshape(2, 2, 4, 2, 2 * rows, 8 * cols)
    right = lax.dynamic_index_in_dim(right, lax.axis_index("core"), 3, keepdims=False)
    mixed = jnp.einsum("hik,zhwjk->iwzj", left, right, preferred_element_type=jnp.float32)
    mixed = mixed.astype(jnp.bfloat16).reshape(16, rows, 8, cols).transpose(0, 2, 1, 3)
    mixed = exchange(mixed.reshape(128, rows, cols), OUT_GROUP)
    mixed = mixed.transpose(1, 2, 0).astype(jnp.float32)
    first = finish(pair, mixed, gating, omg, omb, owo)

    both, gating = project_all(first, ig, ib, iwi)
    both = exchange(both, IN_GROUP).reshape(32, 4, 2, rows, cols)
    both = both.transpose(2, 0, 3, 1, 4).reshape(2, 32 * rows, 4 * cols)
    left = lax.all_gather(both[0], ("xh", "core"), axis=0)
    left = left.reshape(2, 2, 32 * rows, 2, 2, cols)
    mixed = jnp.einsum("xhkylc,kj->yxlhcj", left, both[1], preferred_element_type=jnp.float32)
    mixed = mixed.astype(jnp.bfloat16).reshape(32, rows, 4, cols).transpose(0, 2, 1, 3)
    mixed = exchange(mixed.reshape(128, rows, cols), IN_GROUP)
    mixed = mixed.transpose(1, 2, 0).astype(jnp.float32)
    return finish(first, mixed, gating, img, imb, iwo)


def solution(mesh):
    fine = Mesh(mesh.devices.reshape(4, 2, 4, 2, 2, 2, 2), AXES)
    return jax.shard_map(
        shards,
        mesh=fine,
        in_specs=(P(ROW, COL, None),) + (P(),) * 12,
        out_specs=P(ROW, COL, None),
        check_vma=False,
    )
```

```python
import jax
import jax.numpy as jnp
from jax import lax
from jax.experimental import pallas as pl
from jax.experimental.pallas import tpu as pltpu
from jax.sharding import Mesh, PartitionSpec as P

CH = 128
EPSILON = 1e-05
ROWS, COLS = 14, 28
F32, BF16 = jnp.float32, jnp.bfloat16

AXES = ("zh", "zl", "ylo", "yhi", "xh", "xl", "core")
ROW, COL = AXES[:3], AXES[3:]
OUT_GROUP = ("yhi", "xh", "xl", "zh", "ylo")
IN_GROUP = ("yhi", "xl", "zh", "zl", "ylo")
OUT_SHAPE, IN_SHAPE = (8, 16), (4, 32)


NT = (((1,), (1,)), ((), ()))
TN = (((0,), (1,)), ((), ()))


def dot(a, b, dims=(((1,), (0,)), ((), ()))):
    return lax.dot_general(a, b, dims, preferred_element_type=F32)


def iota(shape, axis):
    return lax.broadcasted_iota(jnp.int32, shape, axis)


def residue_of_slot(slot):
    inner = slot % 16
    residue = inner % 4 * 4 + inner // 4
    return jnp.where(residue < ROWS, slot // 16 * ROWS + residue, -1)


def transpose_groups(blocks):
    lane = iota(blocks[0].shape, 1)
    low, even = lane < 64, lane // 32 % 2 == 0
    a, b, c, d = blocks
    a, c = jnp.where(low, a, pltpu.roll(c, 64, 1)), jnp.where(low, pltpu.roll(a, 64, 1), c)
    b, d = jnp.where(low, b, pltpu.roll(d, 64, 1)), jnp.where(low, pltpu.roll(b, 64, 1), d)
    a, b = jnp.where(even, a, pltpu.roll(b, 32, 1)), jnp.where(even, pltpu.roll(a, 96, 1), b)
    c, d = jnp.where(even, c, pltpu.roll(d, 32, 1)), jnp.where(even, pltpu.roll(c, 96, 1), d)
    return [a, b, c, d]


def layer_norm(values, gain, bias):
    center = values - jnp.mean(values, axis=-1, keepdims=True)
    spread = jnp.mean(center * center, axis=-1, keepdims=True)
    return center * lax.rsqrt(spread + EPSILON) * gain + bias


def project(q, values, gain, bias, weight, stage, gate):
    normed = layer_norm(values, gain[...], bias[...]).astype(BF16)
    lane = iota((CH, 128), 1)
    valid = (lane // 32 * 4 + q < ROWS) & (residue_of_slot(lane % 32) >= 0)
    for side in range(2):
        opened = dot(weight[:, 2 * side * CH : (2 * side + 1) * CH], normed, TN)
        value = dot(weight[:, (2 * side + 1) * CH : (2 * side + 2) * CH], normed, TN)
        operand = jnp.where(valid, jax.nn.sigmoid(opened) * value, 0.0)
        stage[pl.ds(2 * q + side, CH, stride=8), :] = operand
    gate[128 * q : 128 * (q + 1), :] = jax.nn.sigmoid(dot(normed, weight[:, 4 * CH :]))


def finish(q, pair, mixed, gate, gain, bias, weight):
    values = mixed[pl.ds(q, CH, stride=4), :].T
    normed = layer_norm(values, gain[...], bias[...]).astype(BF16)
    rows = slice(128 * q, 128 * (q + 1))
    return (pair[rows, :].astype(F32) + gate[rows, :] * dot(normed, weight[...])).astype(BF16)


def open_kernel(pair, gain, bias, weight, sent, gate, spread, stage):
    place = (residue_of_slot(iota((32, COLS), 0)) == iota((32, COLS), 1)).astype(BF16)
    for q in range(4):
        parts = [
            dot(place, pair[4 * g + q]) if 4 * g + q < ROWS else jnp.zeros((32, CH), F32)
            for g in range(4)
        ]
        values = jnp.concatenate(parts, axis=0)
        spread[128 * q : 128 * (q + 1), :] = values.astype(BF16)
        project(q, values, gain, bias, weight, stage, gate)
    sent[...] = stage[...].astype(BF16)


def middle_kernel(
    pair, got, gate, mix_gain, mix_bias, weight_out, gain, bias, weight, sent, first, gate_in, mixed, stage
):
    mixed[...] = got[...].astype(F32)
    for q in range(4):
        values = finish(q, pair, mixed, gate, mix_gain, mix_bias, weight_out)
        first[128 * q : 128 * (q + 1), :] = values
        project(q, values.astype(F32), gain, bias, weight, stage, gate_in)
    sent[...] = stage[...].astype(BF16)


def close_kernel(first, got, gate, mix_gain, mix_bias, weight_out, updated, mixed):
    mixed[...] = got[...].astype(F32)
    place = (residue_of_slot(iota((COLS, 32), 1)) == iota((COLS, 32), 0)).astype(BF16)
    for q in range(4):
        values = finish(q, first, mixed, gate, mix_gain, mix_bias, weight_out)
        for g in range(4):
            if 4 * g + q < ROWS:
                updated[4 * g + q] = dot(place, values[32 * g : 32 * (g + 1)]).astype(BF16)


def split_kernel_out(got, left, right, stage, order):
    cols, rows = OUT_SHAPE
    size = rows * 8
    for half in range(2):
        lanes = slice(128 * half, 128 * (half + 1))
        first = 4 * half
        blocks = [got[size * (first + c) : size * (first + c + 1), :].astype(F32) for c in range(4)]
        for g, block in enumerate(transpose_groups(blocks)):
            stage[...] = block
            left[64 * g : 64 * (g + 1), lanes] = stage[pl.ds(0, 64, stride=2), :].astype(BF16)
            order[pl.ds(g, 64, stride=4), :] = stage[pl.ds(1, 64, stride=2), :]
        for zh in range(4):
            for yb in range(2):
                source, target = 32 * (2 * zh + yb), 32 * (4 * yb + zh)
                right[target : target + 32, lanes] = order[source : source + 32, :].astype(BF16)


def product_kernel_out(left, right, sent):
    core = lax.axis_index("core")
    for zl in range(2):
        mixed = jnp.zeros((256, 128), F32)
        for half in range(2):
            start = pl.multiple_of((2 * zl + half) * 256 + core * 128, 128)
            mixed += dot(left[256 * half : 256 * (half + 1), :], right[pl.ds(start, 128), :], NT)
        blocks = [mixed[64 * g : 64 * (g + 1)] for g in range(4)]
        for zh, block in enumerate(transpose_groups(blocks)):
            target = 64 * (2 * zh + zl)
            sent[target : target + 64, :] = block.astype(BF16)


def split_kernel_in(got, left, right, stage):
    blocks = [got[256 * c : 256 * (c + 1), :].astype(F32) for c in range(4)]
    for g, block in enumerate(transpose_groups(blocks)):
        stage[...] = block
        rows = slice(128 * g, 128 * (g + 1))
        left[:, rows] = stage[pl.ds(0, 128, stride=2), :].T.astype(BF16)
        right[rows, :] = stage[pl.ds(1, 128, stride=2), :].astype(BF16)


def product_kernel_in(left, right, sent, stage):
    for xh in range(2):
        for core in range(2):
            start = 128 * (2 * xh + core)
            mixed = dot(left[start : start + 128, :], right[...])
            for yhi in range(2):
                for xl in range(2):
                    source = 32 * (2 * yhi + xl)
                    target = 32 * (8 * yhi + 4 * xh + 2 * xl + core)
                    stage[target : target + 32, :] = mixed[source : source + 32]
    blocks = [stage[pl.ds(g, 128, stride=4), :] for g in range(4)]
    for c, block in enumerate(transpose_groups(blocks)):
        sent[128 * c : 128 * (c + 1), :] = block.astype(BF16)


def call(kernel, outs, scratch, *operands):
    whole = pl.BlockSpec(memory_space=pltpu.VMEM)
    outs = [jax.ShapeDtypeStruct(shape, kind) for shape, kind in outs]
    return pl.pallas_call(
        kernel,
        out_shape=outs,
        in_specs=[whole] * len(operands),
        out_specs=[whole] * len(outs),
        scratch_shapes=[pltpu.VMEM(shape, F32) for shape in scratch],
        compiler_params=pltpu.CompilerParams(vmem_limit_bytes=32 * 1024 * 1024),
    )(*operands)


def exchange(values, group):
    size = values.shape[0] // 128
    got = lax.all_to_all(values.reshape(128, size, 128), group, 0, 0, tiled=True)
    return got.reshape(values.shape)


def shards(pair, og, ob, owi, omg, omb, owo, ig, ib, iwi, img, imb, iwo):
    og, ob, omg, omb, ig, ib, img, imb = (v.reshape(1, CH) for v in (og, ob, omg, omb, ig, ib, img, imb))
    sent, gate, pair = call(
        open_kernel,
        [((1024, 128), BF16), ((512, CH), F32), ((512, CH), BF16)],
        [(1024, 128)],
        pair, og, ob, owi,
    )
    got = exchange(sent, OUT_GROUP)
    left, right = call(
        split_kernel_out,
        [((256, 256), BF16), ((256, 256), BF16)],
        [(128, 128), (256, 128)],
        got,
    )
    left = lax.all_gather(left, "core", axis=0, tiled=True)
    right = lax.all_gather(right, ("zl", "core"), axis=0, tiled=True)
    (sent,) = call(product_kernel_out, [((512, 128), BF16)], [], left, right)
    got = exchange(sent, OUT_GROUP)
    sent, first, gate = call(
        middle_kernel,
        [((1024, 128), BF16), ((512, CH), BF16), ((512, CH), F32)],
        [(512, 128), (1024, 128)],
        pair, got, gate, omg, omb, owo, ig, ib, iwi,
    )
    got = exchange(sent, IN_GROUP)
    left, right = call(
        split_kernel_in,
        [((128, 512), BF16), ((512, 128), BF16)],
        [(256, 128)],
        got,
    )
    left = lax.all_gather(left, ("xh", "core"), axis=0, tiled=True)
    (sent,) = call(product_kernel_in, [((512, 128), BF16)], [(512, 128)], left, right)
    got = exchange(sent, IN_GROUP)
    (updated,) = call(
        close_kernel,
        [((ROWS, COLS, CH), BF16)],
        [(512, 128)],
        first, got, gate, img, imb, iwo,
    )
    return updated


def solution(mesh):
    fine = Mesh(mesh.devices.reshape(4, 2, 4, 2, 2, 2, 2), AXES)
    return jax.shard_map(
        shards,
        mesh=fine,
        in_specs=(P(ROW, COL, None),) + (P(),) * 12,
        out_specs=P(ROW, COL, None),
        check_vma=False,
    )
```

```python
import jax
import jax.numpy as jnp
from jax import lax
from jax.experimental import pallas as pl
from jax.experimental.pallas import tpu as pltpu
from jax.sharding import Mesh, PartitionSpec as P

CH = 128
EPSILON = 1e-05
ROWS, COLS = 14, 28
F32, BF16 = jnp.float32, jnp.bfloat16

AXES = ("z2", "z1", "z0", "yb", "ya", "yc", "x1", "x0", "core")
ROW, COL = AXES[:5], AXES[5:]
GROUP = ("yc", "yb", "ya", "z2", "z1", "z0", "x0")
SUM_GROUP = ("x1",) + GROUP


NT = (((1,), (1,)), ((), ()))
TN = (((0,), (1,)), ((), ()))


def dot(a, b, dims=(((1,), (0,)), ((), ()))):
    return lax.dot_general(a, b, dims, preferred_element_type=F32)


def iota(shape, axis):
    return lax.broadcasted_iota(jnp.int32, shape, axis)


def residue_of_slot(slot):
    inner = slot % 16
    residue = inner % 4 * 4 + inner // 4
    return jnp.where(residue < ROWS, slot // 16 * ROWS + residue, -1)


def transpose_groups(blocks):
    lane = iota(blocks[0].shape, 1)
    low, even = lane < 64, lane // 32 % 2 == 0
    a, b, c, d = blocks
    a, c = jnp.where(low, a, pltpu.roll(c, 64, 1)), jnp.where(low, pltpu.roll(a, 64, 1), c)
    b, d = jnp.where(low, b, pltpu.roll(d, 64, 1)), jnp.where(low, pltpu.roll(b, 64, 1), d)
    a, b = jnp.where(even, a, pltpu.roll(b, 32, 1)), jnp.where(even, pltpu.roll(a, 96, 1), b)
    c, d = jnp.where(even, c, pltpu.roll(d, 32, 1)), jnp.where(even, pltpu.roll(c, 96, 1), d)
    return [a, b, c, d]


def bits(names, number):
    return {name: number >> (len(names) - 1 - n) & 1 for n, name in enumerate(names)}


def place_in(names, values):
    place = 0
    for name in names:
        place = 2 * place + values[name]
    return place


def gather_blocks(got):
    values = got[...].astype(F32)
    blocks = []
    for c in range(4):
        places = [place_in(GROUP, {**bits(ROW, r), **bits(("yc", "x0"), c)}) for r in range(32)]
        blocks.append(jnp.concatenate([values[8 * p : 8 * (p + 1)] for p in places], axis=0))
    return transpose_groups(blocks)


def scatter_block(block, stage, group, row_names, col_bits):
    for n in range(block.shape[0] // 4):
        place = place_in(group, {**bits(row_names, n), **col_bits})
        stage[4 * place : 4 * (place + 1), :] = block[4 * n : 4 * (n + 1)]


def layer_norm(values, gain, bias):
    center = values - jnp.mean(values, axis=-1, keepdims=True)
    spread = jnp.mean(center * center, axis=-1, keepdims=True)
    return center * lax.rsqrt(spread + EPSILON) * gain + bias


def project(q, values, gain, bias, weight, stage, gate):
    normed = layer_norm(values, gain, bias).astype(BF16)
    lane = iota((CH, 128), 1)
    valid = (lane // 32 * 4 + q < ROWS) & (residue_of_slot(lane % 32) >= 0)
    for side in range(2):
        opened = dot(weight[:, 2 * side * CH : (2 * side + 1) * CH], normed, TN)
        value = dot(weight[:, (2 * side + 1) * CH : (2 * side + 2) * CH], normed, TN)
        operand = jnp.where(valid, jax.nn.sigmoid(opened) * value, 0.0)
        stage[pl.ds(2 * q + side, CH, stride=8), :] = operand
    gate[128 * q : 128 * (q + 1), :] = jax.nn.sigmoid(dot(normed, weight[:, 4 * CH :]))


def finish(q, pair, mixed, gate, gain, bias, weight):
    values = mixed[pl.ds(q, CH, stride=4), :].T
    normed = layer_norm(values, gain, bias).astype(BF16)
    rows = slice(128 * q, 128 * (q + 1))
    return (pair[rows, :].astype(F32) + gate[rows, :] * dot(normed, weight[...])).astype(BF16)


def open_kernel(*refs):
    pair_in, weight_in, params = refs[0], refs[1], refs[2:10]
    sent, gate, spread, vectors, pair, weight, stage, sems = refs[10:]
    copies = [
        pltpu.make_async_copy(pair_in, pair, sems.at[8]),
        pltpu.make_async_copy(weight_in, weight, sems.at[9]),
    ]
    copies += [
        pltpu.make_async_copy(param, vectors.at[pl.ds(n, 1), :], sems.at[n])
        for n, param in enumerate(params)
    ]
    for copy in copies:
        copy.start()
    for copy in copies:
        copy.wait()
    place = (residue_of_slot(iota((32, COLS), 0)) == iota((32, COLS), 1)).astype(BF16)
    for q in range(4):
        parts = [
            dot(place, pair[4 * g + q]) if 4 * g + q < ROWS else jnp.zeros((32, CH), F32)
            for g in range(4)
        ]
        values = jnp.concatenate(parts, axis=0)
        spread[128 * q : 128 * (q + 1), :] = values.astype(BF16)
        project(q, values, vectors[0:1, :], vectors[1:2, :], weight, stage, gate)
    sent[...] = stage[...].astype(BF16)


def middle_kernel(pair, got, gate, vectors, weight_out, weight, sent, first, gate_in, mixed, stage):
    mixed[...] = got[:512, :].astype(F32) + got[512:, :].astype(F32)
    for q in range(4):
        values = finish(q, pair, mixed, gate, vectors[2:3, :], vectors[3:4, :], weight_out)
        first[128 * q : 128 * (q + 1), :] = values
        project(q, values.astype(F32), vectors[4:5, :], vectors[5:6, :], weight, stage, gate_in)
    sent[...] = stage[...].astype(BF16)


def close_kernel(first, got, gate, vectors, weight_out, updated, mixed):
    mixed[...] = got[...].astype(F32)
    place = (residue_of_slot(iota((COLS, 32), 1)) == iota((COLS, 32), 0)).astype(BF16)
    for q in range(4):
        values = finish(q, first, mixed, gate, vectors[6:7, :], vectors[7:8, :], weight_out)
        for g in range(4):
            if 4 * g + q < ROWS:
                updated[4 * g + q] = dot(place, values[32 * g : 32 * (g + 1)]).astype(BF16)


def split_kernel_out(got, both, stage, order):
    for g, block in enumerate(gather_blocks(got)):
        stage[...] = block
        both[128 * g : 128 * (g + 1), :] = stage[pl.ds(0, 128, stride=2), :].astype(BF16)
        order[pl.ds(g, 128, stride=4), :] = stage[pl.ds(1, 128, stride=2), :]
    for c in range(16):
        target = 512 + 32 * (c % 2 * 8 + c // 2)
        both[target : target + 32, :] = order[32 * c : 32 * (c + 1), :].astype(BF16)


def product_kernel_out(both, sent, stage):
    core = lax.axis_index("core")
    mixed = jnp.zeros((512, 256), F32)
    for part in range(2):
        start = pl.multiple_of(1024 * part + 512 + 256 * core, 256)
        mixed += dot(both[1024 * part : 1024 * part + 512, :], both[pl.ds(start, 256), :], NT)
    for yc in range(2):
        blocks = [mixed[128 * g : 128 * (g + 1), 128 * yc : 128 * (yc + 1)] for g in range(4)]
        for c, block in enumerate(transpose_groups(blocks)):
            scatter_block(block, stage, SUM_GROUP, ROW, {"yc": yc, **bits(("x1", "x0"), c)})
    sent[...] = stage[...].astype(BF16)


def split_kernel_in(got, left, right, stage):
    for g, block in enumerate(gather_blocks(got)):
        stage[...] = block
        rows = slice(128 * g, 128 * (g + 1))
        left[:, rows] = stage[pl.ds(0, 128, stride=2), :].T.astype(BF16)
        right[rows, :] = stage[pl.ds(1, 128, stride=2), :].astype(BF16)


def product_kernel_in(left, right, sent, stage, packed):
    stage[...] = dot(left[...], right[...])
    blocks = [stage[pl.ds(g, 128, stride=4), :] for g in range(4)]
    for c, block in enumerate(transpose_groups(blocks)):
        scatter_block(block, packed, GROUP, ("z1", "yb", "z2", "z0", "ya"), bits(("yc", "x0"), c))
    sent[...] = packed[...].astype(BF16)


def call(kernel, outs, scratch, *operands, hbm=False):
    whole = pl.BlockSpec(memory_space=pltpu.VMEM)
    outs = [jax.ShapeDtypeStruct(shape, kind) for shape, kind in outs]
    return pl.pallas_call(
        kernel,
        out_shape=outs,
        in_specs=[pl.BlockSpec(memory_space=pltpu.HBM) if hbm else whole] * len(operands),
        out_specs=[whole] * len(outs),
        scratch_shapes=[pltpu.VMEM(s, F32) if isinstance(s, tuple) else s for s in scratch],
        compiler_params=pltpu.CompilerParams(vmem_limit_bytes=32 * 1024 * 1024),
    )(*operands)


def exchange(values, group, size):
    got = lax.all_to_all(values.reshape(-1, size, 128), group, 0, 0, tiled=True)
    return got.reshape(values.shape)


def shards(pair, og, ob, owi, omg, omb, owo, ig, ib, iwi, img, imb, iwo):
    params = [v.reshape(1, CH) for v in (og, ob, omg, omb, ig, ib, img, imb)]
    sent, gate, pair, vectors = call(
        open_kernel,
        [((1024, 128), BF16), ((512, CH), F32), ((512, CH), BF16), ((8, CH), F32)],
        [
            pltpu.VMEM(pair.shape, BF16),
            pltpu.VMEM(owi.shape, BF16),
            (1024, 128),
            pltpu.SemaphoreType.DMA((10,)),
        ],
        pair, owi, *params,
        hbm=True,
    )
    got = exchange(sent, GROUP, 8)
    (both,) = call(split_kernel_out, [((1024, 128), BF16)], [(256, 128), (512, 128)], got)
    both = lax.all_gather(both, "core", axis=0, tiled=True)
    (sent,) = call(product_kernel_out, [((1024, 128), BF16)], [(1024, 128)], both)
    got = exchange(sent, SUM_GROUP, 4)
    sent, first, gate = call(
        middle_kernel,
        [((1024, 128), BF16), ((512, CH), BF16), ((512, CH), F32)],
        [(512, 128), (1024, 128)],
        pair, got, gate, vectors, owo, iwi,
    )
    got = exchange(sent, GROUP, 8)
    left, right = call(
        split_kernel_in,
        [((128, 512), BF16), ((512, 128), BF16)],
        [(256, 128)],
        got,
    )
    left = lax.all_gather(left, ("x1", "core"), axis=0, tiled=True)
    (sent,) = call(
        product_kernel_in, [((512, 128), BF16)], [(512, 128), (512, 128)], left, right
    )
    got = exchange(sent, GROUP, 4)
    (updated,) = call(
        close_kernel,
        [((ROWS, COLS, CH), BF16)],
        [(512, 128)],
        first, got, gate, vectors, iwo,
    )
    return updated


def solution(mesh):
    fine = Mesh(mesh.devices.reshape((2,) * 9), AXES)
    return jax.shard_map(
        shards,
        mesh=fine,
        in_specs=(P(ROW, COL, None),) + (P(),) * 12,
        out_specs=P(ROW, COL, None),
        check_vma=False,
    )
```

```python
import jax
import jax.numpy as jnp
from jax import lax
from jax.experimental import pallas as pl
from jax.experimental.pallas import tpu as pltpu
from jax.sharding import Mesh, PartitionSpec as P

CH = 128
EPSILON = 1e-05
ROWS, COLS = 14, 28
F32, BF16 = jnp.float32, jnp.bfloat16

AXES = ("z2", "z1", "z0", "yb", "ya", "yc", "x1", "x0", "core")
ROW, COL = AXES[:5], AXES[5:]
GROUP = ("yc", "yb", "ya", "z0", "z1", "z2", "x0")
SUM_GROUP = GROUP + ("x1",)


NT = (((1,), (1,)), ((), ()))


def dot(a, b, dims=(((1,), (0,)), ((), ()))):
    return lax.dot_general(a, b, dims, preferred_element_type=F32)


def iota(shape, axis):
    return lax.broadcasted_iota(jnp.int32, shape, axis)


def residue_of_slot(slot):
    inner = slot % 16
    residue = inner % 4 * 4 + inner // 4
    return jnp.where(residue < ROWS, slot // 16 * ROWS + residue, -1)


def transpose_groups(blocks):
    lane = iota(blocks[0].shape, 1)
    low, even = lane < 64, lane // 32 % 2 == 0
    a, b, c, d = blocks
    a, c = jnp.where(low, a, pltpu.roll(c, 64, 1)), jnp.where(low, pltpu.roll(a, 64, 1), c)
    b, d = jnp.where(low, b, pltpu.roll(d, 64, 1)), jnp.where(low, pltpu.roll(b, 64, 1), d)
    a, b = jnp.where(even, a, pltpu.roll(b, 32, 1)), jnp.where(even, pltpu.roll(a, 96, 1), b)
    c, d = jnp.where(even, c, pltpu.roll(d, 32, 1)), jnp.where(even, pltpu.roll(c, 96, 1), d)
    return [a, b, c, d]


def bits(names, number):
    return {name: number >> (len(names) - 1 - n) & 1 for n, name in enumerate(names)}


def place_in(names, values):
    place = 0
    for name in names:
        place = 2 * place + values[name]
    return place


def gather_blocks(got):
    values = got[...].astype(F32)
    blocks = []
    for c in range(4):
        places = [place_in(GROUP, {**bits(ROW, r), **bits(("yc", "x0"), c)}) for r in range(32)]
        blocks.append(jnp.concatenate([values[8 * p : 8 * (p + 1)] for p in places], axis=0))
    return transpose_groups(blocks)


def scatter_block(block, stage, group, row_names, col_bits):
    for n in range(block.shape[0] // 4):
        place = place_in(group, {**bits(row_names, n), **col_bits})
        stage[4 * place : 4 * (place + 1), :] = block[4 * n : 4 * (n + 1)]


def layer_norm(values, gain, bias):
    center = values - jnp.mean(values, axis=0, keepdims=True)
    spread = jnp.mean(center * center, axis=0, keepdims=True)
    return center * lax.rsqrt(spread + EPSILON) * gain + bias


def columns(vectors, *rows):
    turned = vectors.T
    return [jnp.broadcast_to(turned[:, row : row + 1], (CH, 128)) for row in rows]


def project(q, values, gain, bias, weight, stage, gate):
    normed = layer_norm(values, gain, bias).astype(BF16)
    projected = dot(weight, normed)
    lane = iota((CH, 128), 1)
    valid = (lane // 32 * 4 + q < ROWS) & (residue_of_slot(lane % 32) >= 0)
    for side in range(2):
        opened = projected[2 * side * CH : (2 * side + 1) * CH]
        value = projected[(2 * side + 1) * CH : (2 * side + 2) * CH]
        operand = jnp.where(valid, jax.nn.sigmoid(opened) * value, 0.0)
        stage[pl.ds(2 * q + side, CH, stride=8), :] = operand
    gate[:CH, 128 * q : 128 * (q + 1)] = jax.nn.sigmoid(projected[4 * CH :])


def finish(q, pair, mixed, gate, gain, bias, weight):
    normed = layer_norm(mixed, gain, bias).astype(BF16)
    lanes = slice(128 * q, 128 * (q + 1))
    return (pair[:, lanes].astype(F32) + gate[:CH, lanes] * dot(weight, normed)).astype(BF16)


def open_kernel(*refs):
    pair_in, weight_in, params = refs[0], refs[1], refs[2:10]
    sent, gate, spread, pair, weight, stage, sems = refs[10:]
    pair_copy = pltpu.make_async_copy(pair_in, pair, sems.at[8])
    copies = [pltpu.make_async_copy(weight_in, weight, sems.at[9])]
    copies += [
        pltpu.make_async_copy(param, gate.at[pl.ds(CH + n, 1), pl.ds(0, CH)], sems.at[n])
        for n, param in enumerate(params)
    ]
    for copy in [pair_copy, *copies]:
        copy.start()
    pair_copy.wait()
    place = (residue_of_slot(iota((32, COLS), 0)) == iota((32, COLS), 1)).astype(BF16)
    values = []
    for q in range(4):
        parts = [
            dot(place, pair[4 * g + q]) if 4 * g + q < ROWS else jnp.zeros((32, CH), F32)
            for g in range(4)
        ]
        values.append(jnp.concatenate(parts, axis=0).T)
        spread[:, 128 * q : 128 * (q + 1)] = values[q].astype(BF16)
    for copy in copies:
        copy.wait()
    gain, bias = columns(gate[CH:, :CH], 0, 1)
    turned = weight[...].T
    for q in range(4):
        project(q, values[q], gain, bias, turned, stage, gate)
    sent[...] = stage[...].astype(BF16)


def middle_kernel(pair, got, gate, weight_out, weight, sent, first, gate_in, mixed, stage):
    mixed[...] = got[...].astype(F32)
    vectors = gate[CH:, :CH]
    gate_in[CH:, :CH] = vectors
    mix_gain, mix_bias, gain, bias = columns(vectors, 2, 3, 4, 5)
    turned_out, turned = weight_out[...].T, weight[...].T
    for q in range(4):
        values = mixed[pl.ds(q, CH, stride=8), :] + mixed[pl.ds(4 + q, CH, stride=8), :]
        values = finish(q, pair, values, gate, mix_gain, mix_bias, turned_out)
        first[:, 128 * q : 128 * (q + 1)] = values
        project(q, values.astype(F32), gain, bias, turned, stage, gate_in)
    sent[...] = stage[...].astype(BF16)


def close_kernel(first, got, gate, weight_out, updated, mixed):
    mixed[...] = got[...].astype(F32)
    gain, bias = columns(gate[CH:, :CH], 6, 7)
    turned = weight_out[...].T
    row, lane = iota((128, 128), 0), iota((128, 128), 1)
    place = (row // 32 == lane // 32) & (residue_of_slot(lane % 32) == row % 32)
    place = place.astype(F32).astype(BF16)
    for q in range(4):
        values = mixed[pl.ds(q, CH, stride=4), :]
        values = finish(q, first, values, gate, gain, bias, turned)
        values = dot(place, values, NT).astype(BF16)
        for g in range(4):
            if 4 * g + q < ROWS:
                updated[4 * g + q] = values[32 * g : 32 * g + COLS]


def split_kernel_out(got, both, stage, order):
    for g, block in enumerate(gather_blocks(got)):
        stage[...] = block
        both[128 * g : 128 * (g + 1), :] = stage[pl.ds(0, 128, stride=2), :].astype(BF16)
        order[pl.ds(g, 128, stride=4), :] = stage[pl.ds(1, 128, stride=2), :]
    for c in range(16):
        target = 512 + 32 * (c % 2 * 8 + c // 2)
        both[target : target + 32, :] = order[32 * c : 32 * (c + 1), :].astype(BF16)


def product_kernel_out(both, sent, stage):
    core = lax.axis_index("core")
    mixed = jnp.zeros((512, 256), F32)
    for part in range(2):
        start = pl.multiple_of(1024 * part + 512 + 256 * core, 256)
        mixed += dot(both[1024 * part : 1024 * part + 512, :], both[pl.ds(start, 256), :], NT)
    for yc in range(2):
        blocks = [mixed[128 * g : 128 * (g + 1), 128 * yc : 128 * (yc + 1)] for g in range(4)]
        for c, block in enumerate(transpose_groups(blocks)):
            scatter_block(block, stage, SUM_GROUP, ROW, {"yc": yc, **bits(("x1", "x0"), c)})
    sent[...] = stage[...].astype(BF16)


def split_kernel_in(got, left, right, stage):
    for g, block in enumerate(gather_blocks(got)):
        stage[...] = block
        rows = slice(128 * g, 128 * (g + 1))
        left[:, rows] = stage[pl.ds(0, 128, stride=2), :].T.astype(BF16)
        right[rows, :] = stage[pl.ds(1, 128, stride=2), :].astype(BF16)


def product_kernel_in(left, right, sent, stage, packed):
    stage[...] = dot(left[...], right[...])
    blocks = [stage[pl.ds(g, 128, stride=4), :] for g in range(4)]
    for c, block in enumerate(transpose_groups(blocks)):
        scatter_block(block, packed, GROUP, ("z1", "yb", "z2", "z0", "ya"), bits(("yc", "x0"), c))
    sent[...] = packed[...].astype(BF16)


def call(kernel, outs, scratch, *operands, hbm=False):
    whole = pl.BlockSpec(memory_space=pltpu.VMEM)
    outs = [jax.ShapeDtypeStruct(shape, kind) for shape, kind in outs]
    return pl.pallas_call(
        kernel,
        out_shape=outs,
        in_specs=[pl.BlockSpec(memory_space=pltpu.HBM) if hbm else whole] * len(operands),
        out_specs=[whole] * len(outs),
        scratch_shapes=[pltpu.VMEM(s, F32) if isinstance(s, tuple) else s for s in scratch],
        compiler_params=pltpu.CompilerParams(vmem_limit_bytes=(62 if hbm else 32) * 1024 * 1024),
    )(*operands)


def exchange(values, group, size):
    got = lax.all_to_all(values.reshape(-1, size, 128), group, 0, 0, tiled=True)
    return got.reshape(values.shape)


def shards(pair, og, ob, owi, omg, omb, owo, ig, ib, iwi, img, imb, iwo):
    params = [v.reshape(1, CH) for v in (og, ob, omg, omb, ig, ib, img, imb)]
    sent, gate, pair = call(
        open_kernel,
        [((1024, 128), BF16), ((CH + 8, 512), F32), ((CH, 512), BF16)],
        [
            pltpu.VMEM(pair.shape, BF16),
            pltpu.VMEM(owi.shape, BF16),
            (1024, 128),
            pltpu.SemaphoreType.DMA((10,)),
        ],
        pair, owi, *params,
        hbm=True,
    )
    got = exchange(sent, GROUP, 8)
    (both,) = call(split_kernel_out, [((1024, 128), BF16)], [(256, 128), (512, 128)], got)
    both = lax.all_gather(both, "core", axis=0, tiled=True)
    (sent,) = call(product_kernel_out, [((1024, 128), BF16)], [(1024, 128)], both)
    got = exchange(sent, SUM_GROUP, 4)
    sent, first, gate = call(
        middle_kernel,
        [((1024, 128), BF16), ((CH, 512), BF16), ((CH + 8, 512), F32)],
        [(1024, 128), (1024, 128)],
        pair, got, gate, owo, iwi,
    )
    got = exchange(sent, GROUP, 8)
    left, right = call(
        split_kernel_in,
        [((128, 512), BF16), ((512, 128), BF16)],
        [(256, 128)],
        got,
    )
    left = lax.all_gather(left, ("x1", "core"), axis=0, tiled=True)
    (sent,) = call(
        product_kernel_in, [((512, 128), BF16)], [(512, 128), (512, 128)], left, right
    )
    got = exchange(sent, GROUP, 4)
    (updated,) = call(
        close_kernel,
        [((ROWS, COLS, CH), BF16)],
        [(512, 128)],
        first, got, gate, iwo,
    )
    return updated


def solution(mesh):
    fine = Mesh(mesh.devices.reshape((2,) * 9), AXES)
    return jax.shard_map(
        shards,
        mesh=fine,
        in_specs=(P(ROW, COL, None),) + (P(),) * 12,
        out_specs=P(ROW, COL, None),
        check_vma=False,
    )
```

```python
import jax
import jax.numpy as jnp
from jax import lax
from jax.experimental import pallas as pl
from jax.experimental.pallas import tpu as pltpu
from jax.sharding import Mesh, PartitionSpec as P

CH = 128
EPSILON = 1e-05
ROWS, COLS = 14, 28
F32, BF16 = jnp.float32, jnp.bfloat16

AXES = ("z2", "z1", "z0", "yb", "ya", "yc", "x1", "x0", "core")
ROW, COL = AXES[:5], AXES[5:]
OUT_GROUP = ("yb", "ya", "z0", "z1", "z2", "x1", "x0")
SUM_GROUP = OUT_GROUP + ("yc",)
IN_GROUP = ("yc", "yb", "ya", "z0", "z1", "z2", "x0")


NT = (((1,), (1,)), ((), ()))


def dot(a, b, dims=(((1,), (0,)), ((), ()))):
    return lax.dot_general(a, b, dims, preferred_element_type=F32)


def iota(shape, axis):
    return lax.broadcasted_iota(jnp.int32, shape, axis)


def residue_of_slot(slot):
    inner = slot % 16
    residue = inner % 4 * 4 + inner // 4
    return jnp.where(residue < ROWS, slot // 16 * ROWS + residue, -1)


def transpose_groups(blocks):
    lane = iota(blocks[0].shape, 1)
    low, even = lane < 64, lane // 32 % 2 == 0
    a, b, c, d = blocks
    a, c = jnp.where(low, a, pltpu.roll(c, 64, 1)), jnp.where(low, pltpu.roll(a, 64, 1), c)
    b, d = jnp.where(low, b, pltpu.roll(d, 64, 1)), jnp.where(low, pltpu.roll(b, 64, 1), d)
    a, b = jnp.where(even, a, pltpu.roll(b, 32, 1)), jnp.where(even, pltpu.roll(a, 96, 1), b)
    c, d = jnp.where(even, c, pltpu.roll(d, 32, 1)), jnp.where(even, pltpu.roll(c, 96, 1), d)
    return [a, b, c, d]


def bits(names, number):
    return {name: number >> (len(names) - 1 - n) & 1 for n, name in enumerate(names)}


def place_in(names, values):
    place = 0
    for name in names:
        place = 2 * place + values[name]
    return place


def gather_blocks(got, group, col_names):
    values = got[...].astype(F32)
    blocks = []
    for c in range(4):
        places = [place_in(group, {**bits(ROW, r), **bits(col_names, c)}) for r in range(32)]
        blocks.append(jnp.concatenate([values[8 * p : 8 * (p + 1)] for p in places], axis=0))
    return transpose_groups(blocks)


def scatter_block(block, stage, group, row_names, col_bits):
    for n in range(block.shape[0] // 4):
        place = place_in(group, {**bits(row_names, n), **col_bits})
        stage[4 * place : 4 * (place + 1), :] = block[4 * n : 4 * (n + 1)]


def layer_norm(values, gain, bias):
    center = values - jnp.mean(values, axis=0, keepdims=True)
    spread = jnp.mean(center * center, axis=0, keepdims=True)
    return center * lax.rsqrt(spread + EPSILON) * gain + bias


def columns(vectors, *rows):
    turned = vectors.T
    return [jnp.broadcast_to(turned[:, row : row + 1], (CH, 128)) for row in rows]


def project(q, values, gain, bias, weight, stage, gate):
    normed = layer_norm(values, gain, bias).astype(BF16)
    projected = dot(weight, normed)
    lane = iota((CH, 128), 1)
    valid = (lane // 32 * 4 + q < ROWS) & (residue_of_slot(lane % 32) >= 0)
    for side in range(2):
        opened = projected[2 * side * CH : (2 * side + 1) * CH]
        value = projected[(2 * side + 1) * CH : (2 * side + 2) * CH]
        operand = jnp.where(valid, jax.nn.sigmoid(opened) * value, 0.0)
        stage[pl.ds(2 * q + side, CH, stride=8), :] = operand
    gate[:CH, 128 * q : 128 * (q + 1)] = jax.nn.sigmoid(projected[4 * CH :])


def finish(q, pair, mixed, gate, gain, bias, weight):
    normed = layer_norm(mixed, gain, bias).astype(BF16)
    lanes = slice(128 * q, 128 * (q + 1))
    return (pair[:, lanes].astype(F32) + gate[:CH, lanes] * dot(weight, normed)).astype(BF16)


def open_kernel(*refs):
    pair_in, weight_in, params = refs[0], refs[1], refs[2:10]
    sent, gate, spread, pair, weight, stage, sems = refs[10:]
    pair_copy = pltpu.make_async_copy(pair_in, pair, sems.at[8])
    copies = [pltpu.make_async_copy(weight_in, weight, sems.at[9])]
    copies += [
        pltpu.make_async_copy(param, gate.at[pl.ds(CH + n, 1), pl.ds(0, CH)], sems.at[n])
        for n, param in enumerate(params)
    ]
    for copy in [pair_copy, *copies]:
        copy.start()
    pair_copy.wait()
    place = (residue_of_slot(iota((32, COLS), 0)) == iota((32, COLS), 1)).astype(BF16)
    values = []
    for q in range(4):
        parts = [
            dot(place, pair[4 * g + q]) if 4 * g + q < ROWS else jnp.zeros((32, CH), F32)
            for g in range(4)
        ]
        values.append(jnp.concatenate(parts, axis=0).T)
        spread[:, 128 * q : 128 * (q + 1)] = values[q].astype(BF16)
    for copy in copies:
        copy.wait()
    gain, bias = columns(gate[CH:, :CH], 0, 1)
    turned = weight[...].T
    for q in range(4):
        project(q, values[q], gain, bias, turned, stage, gate)
    sent[...] = stage[...].astype(BF16)


def middle_kernel(pair, got, gate, weight_out, weight, sent, first, gate_in, mixed, stage):
    mixed[...] = got[...].astype(F32)
    vectors = gate[CH:, :CH]
    gate_in[CH:, :CH] = vectors
    mix_gain, mix_bias, gain, bias = columns(vectors, 2, 3, 4, 5)
    turned_out, turned = weight_out[...].T, weight[...].T
    for q in range(4):
        values = mixed[pl.ds(q, CH, stride=8), :] + mixed[pl.ds(4 + q, CH, stride=8), :]
        values = finish(q, pair, values, gate, mix_gain, mix_bias, turned_out)
        first[:, 128 * q : 128 * (q + 1)] = values
        project(q, values.astype(F32), gain, bias, turned, stage, gate_in)
    sent[...] = stage[...].astype(BF16)


def close_kernel(first, got, gate, weight_out, updated, mixed):
    mixed[...] = got[...].astype(F32)
    gain, bias = columns(gate[CH:, :CH], 6, 7)
    turned = weight_out[...].T
    row, lane = iota((128, 128), 0), iota((128, 128), 1)
    place = (row // 32 == lane // 32) & (residue_of_slot(lane % 32) == row % 32)
    place = place.astype(F32).astype(BF16)
    for q in range(4):
        values = mixed[pl.ds(q, CH, stride=4), :]
        values = finish(q, first, values, gate, gain, bias, turned)
        values = dot(place, values, NT).astype(BF16)
        for g in range(4):
            if 4 * g + q < ROWS:
                updated[4 * g + q] = values[32 * g : 32 * g + COLS]


def split_kernel_out(got, both, stage, order):
    for g, block in enumerate(gather_blocks(got, OUT_GROUP, ("x1", "x0"))):
        stage[...] = block
        both[128 * g : 128 * (g + 1), :] = stage[pl.ds(0, 128, stride=2), :].astype(BF16)
        order[pl.ds(g, 128, stride=4), :] = stage[pl.ds(1, 128, stride=2), :]
    for c in range(16):
        target = 512 + 32 * (c % 2 * 8 + c // 2)
        both[target : target + 32, :] = order[32 * c : 32 * (c + 1), :].astype(BF16)


def product_kernel_out(both, sent, stage):
    core = lax.axis_index("core")
    mixed = jnp.zeros((512, 256), F32)
    for part in range(2):
        start = pl.multiple_of(1024 * part + 512 + 256 * core, 256)
        mixed += dot(both[1024 * part : 1024 * part + 512, :], both[pl.ds(start, 256), :], NT)
    for yc in range(2):
        blocks = [mixed[128 * g : 128 * (g + 1), 128 * yc : 128 * (yc + 1)] for g in range(4)]
        for c, block in enumerate(transpose_groups(blocks)):
            scatter_block(block, stage, SUM_GROUP, ROW, {"yc": yc, **bits(("x1", "x0"), c)})
    sent[...] = stage[...].astype(BF16)


def split_kernel_in(got, left, right, stage):
    for g, block in enumerate(gather_blocks(got, IN_GROUP, ("yc", "x0"))):
        stage[...] = block
        rows = slice(128 * g, 128 * (g + 1))
        left[:, rows] = stage[pl.ds(0, 128, stride=2), :].T.astype(BF16)
        right[rows, :] = stage[pl.ds(1, 128, stride=2), :].astype(BF16)


def product_kernel_in(left, right, sent, stage, packed):
    stage[...] = dot(left[...], right[...])
    blocks = [stage[pl.ds(g, 128, stride=4), :] for g in range(4)]
    for c, block in enumerate(transpose_groups(blocks)):
        scatter_block(block, packed, IN_GROUP, ("z1", "yb", "z2", "z0", "ya"), bits(("yc", "x0"), c))
    sent[...] = packed[...].astype(BF16)


def call(kernel, outs, scratch, *operands, hbm=False):
    whole = pl.BlockSpec(memory_space=pltpu.VMEM)
    outs = [jax.ShapeDtypeStruct(shape, kind) for shape, kind in outs]
    return pl.pallas_call(
        kernel,
        out_shape=outs,
        in_specs=[pl.BlockSpec(memory_space=pltpu.HBM) if hbm else whole] * len(operands),
        out_specs=[whole] * len(outs),
        scratch_shapes=[pltpu.VMEM(s, F32) if isinstance(s, tuple) else s for s in scratch],
        compiler_params=pltpu.CompilerParams(vmem_limit_bytes=(62 if hbm else 32) * 1024 * 1024),
    )(*operands)


def exchange(values, group, size):
    got = lax.all_to_all(values.reshape(-1, size, 128), group, 0, 0, tiled=True)
    return got.reshape(values.shape)


def shards(pair, og, ob, owi, omg, omb, owo, ig, ib, iwi, img, imb, iwo):
    params = [v.reshape(1, CH) for v in (og, ob, omg, omb, ig, ib, img, imb)]
    sent, gate, pair = call(
        open_kernel,
        [((1024, 128), BF16), ((CH + 8, 512), F32), ((CH, 512), BF16)],
        [
            pltpu.VMEM(pair.shape, BF16),
            pltpu.VMEM(owi.shape, BF16),
            (1024, 128),
            pltpu.SemaphoreType.DMA((10,)),
        ],
        pair, owi, *params,
        hbm=True,
    )
    got = exchange(sent, OUT_GROUP, 8)
    (both,) = call(split_kernel_out, [((1024, 128), BF16)], [(256, 128), (512, 128)], got)
    both = lax.all_gather(both, "core", axis=0, tiled=True)
    (sent,) = call(product_kernel_out, [((1024, 128), BF16)], [(1024, 128)], both)
    got = exchange(sent, SUM_GROUP, 4)
    sent, first, gate = call(
        middle_kernel,
        [((1024, 128), BF16), ((CH, 512), BF16), ((CH + 8, 512), F32)],
        [(1024, 128), (1024, 128)],
        pair, got, gate, owo, iwi,
    )
    got = exchange(sent, IN_GROUP, 8)
    left, right = call(
        split_kernel_in,
        [((128, 512), BF16), ((512, 128), BF16)],
        [(256, 128)],
        got,
    )
    left = lax.all_gather(left, ("x1", "core"), axis=0, tiled=True)
    (sent,) = call(
        product_kernel_in, [((512, 128), BF16)], [(512, 128), (512, 128)], left, right
    )
    got = exchange(sent, IN_GROUP, 4)
    (updated,) = call(
        close_kernel,
        [((ROWS, COLS, CH), BF16)],
        [(512, 128)],
        first, got, gate, iwo,
    )
    return updated


def solution(mesh):
    fine = Mesh(mesh.devices.reshape((2,) * 9), AXES)
    return jax.shard_map(
        shards,
        mesh=fine,
        in_specs=(P(ROW, COL, None),) + (P(),) * 12,
        out_specs=P(ROW, COL, None),
        check_vma=False,
    )
```

```python
import jax
import jax.numpy as jnp
from jax import lax
from jax.experimental import pallas as pl
from jax.experimental.pallas import tpu as pltpu
from jax.sharding import Mesh, PartitionSpec as P

CH = 128
EPSILON = 1e-05
ROWS, COLS = 14, 28
F32, BF16 = jnp.float32, jnp.bfloat16

AXES = ("z2", "z1", "z0", "yb", "ya", "yc", "x1", "x0", "core")
ROW, COL = AXES[:5], AXES[5:]
OUT_GROUP = ("yb", "ya", "z0", "z1", "z2", "x1", "x0")
SUM_GROUP = OUT_GROUP + ("yc",)
IN_GROUP = ('yb', 'ya', 'z2', 'z1', 'z0', 'yc', 'x0')


NT = (((1,), (1,)), ((), ()))


def dot(a, b, dims=(((1,), (0,)), ((), ()))):
    return lax.dot_general(a, b, dims, preferred_element_type=F32)


def iota(shape, axis):
    return lax.broadcasted_iota(jnp.int32, shape, axis)


def residue_of_slot(slot):
    inner = slot % 16
    residue = inner % 4 * 4 + inner // 4
    return jnp.where(residue < ROWS, slot // 16 * ROWS + residue, -1)


def transpose_groups(blocks):
    lane = iota(blocks[0].shape, 1)
    low, even = lane < 64, lane // 32 % 2 == 0
    a, b, c, d = blocks
    a, c = jnp.where(low, a, pltpu.roll(c, 64, 1)), jnp.where(low, pltpu.roll(a, 64, 1), c)
    b, d = jnp.where(low, b, pltpu.roll(d, 64, 1)), jnp.where(low, pltpu.roll(b, 64, 1), d)
    a, b = jnp.where(even, a, pltpu.roll(b, 32, 1)), jnp.where(even, pltpu.roll(a, 96, 1), b)
    c, d = jnp.where(even, c, pltpu.roll(d, 32, 1)), jnp.where(even, pltpu.roll(c, 96, 1), d)
    return [a, b, c, d]


def bits(names, number):
    return {name: number >> (len(names) - 1 - n) & 1 for n, name in enumerate(names)}


def place_in(names, values):
    place = 0
    for name in names:
        place = 2 * place + values[name]
    return place


def gather_blocks(got, group, col_names):
    values = got[...].astype(F32)
    blocks = []
    for c in range(4):
        places = [place_in(group, {**bits(ROW, r), **bits(col_names, c)}) for r in range(32)]
        blocks.append(jnp.concatenate([values[8 * p : 8 * (p + 1)] for p in places], axis=0))
    return transpose_groups(blocks)


def scatter_block(block, stage, group, row_names, col_bits):
    for n in range(block.shape[0] // 4):
        place = place_in(group, {**bits(row_names, n), **col_bits})
        stage[4 * place : 4 * (place + 1), :] = block[4 * n : 4 * (n + 1)]


def layer_norm(values, gain, bias):
    center = values - jnp.mean(values, axis=0, keepdims=True)
    spread = jnp.mean(center * center, axis=0, keepdims=True)
    return center * lax.rsqrt(spread + EPSILON) * gain + bias


def columns(vectors, *rows):
    turned = vectors.T
    return [jnp.broadcast_to(turned[:, row : row + 1], (CH, 128)) for row in rows]


def project(q, values, gain, bias, weight, stage, gate):
    normed = layer_norm(values, gain, bias).astype(BF16)
    projected = dot(weight, normed)
    lane = iota((CH, 128), 1)
    valid = (lane // 32 * 4 + q < ROWS) & (residue_of_slot(lane % 32) >= 0)
    for side in range(2):
        opened = projected[2 * side * CH : (2 * side + 1) * CH]
        value = projected[(2 * side + 1) * CH : (2 * side + 2) * CH]
        operand = jnp.where(valid, jax.nn.sigmoid(opened) * value, 0.0)
        stage[pl.ds(2 * q + side, CH, stride=8), :] = operand
    gate[:CH, 128 * q : 128 * (q + 1)] = jax.nn.sigmoid(projected[4 * CH :])


def finish(q, pair, mixed, gate, gain, bias, weight):
    normed = layer_norm(mixed, gain, bias).astype(BF16)
    lanes = slice(128 * q, 128 * (q + 1))
    return (pair[:, lanes].astype(F32) + gate[:CH, lanes] * dot(weight, normed)).astype(BF16)


def open_kernel(*refs):
    pair_in, weight_in, params = refs[0], refs[1], refs[2:10]
    sent, gate, spread, pair, weight, stage, sems = refs[10:]
    pair_copy = pltpu.make_async_copy(pair_in, pair, sems.at[8])
    copies = [pltpu.make_async_copy(weight_in, weight, sems.at[9])]
    copies += [
        pltpu.make_async_copy(param, gate.at[pl.ds(CH + n, 1), pl.ds(0, CH)], sems.at[n])
        for n, param in enumerate(params)
    ]
    for copy in [pair_copy, *copies]:
        copy.start()
    pair_copy.wait()
    place = (residue_of_slot(iota((32, COLS), 0)) == iota((32, COLS), 1)).astype(BF16)
    values = []
    for q in range(4):
        parts = [
            dot(place, pair[4 * g + q]) if 4 * g + q < ROWS else jnp.zeros((32, CH), F32)
            for g in range(4)
        ]
        values.append(jnp.concatenate(parts, axis=0).T)
        spread[:, 128 * q : 128 * (q + 1)] = values[q].astype(BF16)
    for copy in copies:
        copy.wait()
    gain, bias = columns(gate[CH:, :CH], 0, 1)
    turned = weight[...].T
    for q in range(4):
        project(q, values[q], gain, bias, turned, stage, gate)
    sent[...] = stage[...].astype(BF16)


def middle_kernel(pair, got, gate, weight_out, weight, sent, first, gate_in, mixed, stage):
    mixed[...] = got[...].astype(F32)
    vectors = gate[CH:, :CH]
    gate_in[CH:, :CH] = vectors
    mix_gain, mix_bias, gain, bias = columns(vectors, 2, 3, 4, 5)
    turned_out, turned = weight_out[...].T, weight[...].T
    for q in range(4):
        values = mixed[pl.ds(q, CH, stride=8), :] + mixed[pl.ds(4 + q, CH, stride=8), :]
        values = finish(q, pair, values, gate, mix_gain, mix_bias, turned_out)
        first[:, 128 * q : 128 * (q + 1)] = values
        project(q, values.astype(F32), gain, bias, turned, stage, gate_in)
    sent[...] = stage[...].astype(BF16)


def close_kernel(first, got, gate, weight_out, updated, mixed):
    mixed[...] = got[...].astype(F32)
    gain, bias = columns(gate[CH:, :CH], 6, 7)
    turned = weight_out[...].T
    row, lane = iota((128, 128), 0), iota((128, 128), 1)
    place = (row // 32 == lane // 32) & (residue_of_slot(lane % 32) == row % 32)
    place = place.astype(F32).astype(BF16)
    for q in range(4):
        values = mixed[pl.ds(q, CH, stride=4), :]
        values = finish(q, first, values, gate, gain, bias, turned)
        values = dot(place, values, NT).astype(BF16)
        for g in range(4):
            if 4 * g + q < ROWS:
                updated[4 * g + q] = values[32 * g : 32 * g + COLS]


def split_kernel_out(got, both, stage, order):
    for g, block in enumerate(gather_blocks(got, OUT_GROUP, ("x1", "x0"))):
        stage[...] = block
        both[128 * g : 128 * (g + 1), :] = stage[pl.ds(0, 128, stride=2), :].astype(BF16)
        order[pl.ds(g, 128, stride=4), :] = stage[pl.ds(1, 128, stride=2), :]
    for c in range(16):
        target = 512 + 32 * (c % 2 * 8 + c // 2)
        both[target : target + 32, :] = order[32 * c : 32 * (c + 1), :].astype(BF16)


def product_kernel_out(both, sent, stage):
    core = lax.axis_index("core")
    mixed = jnp.zeros((512, 256), F32)
    for part in range(2):
        start = pl.multiple_of(1024 * part + 512 + 256 * core, 256)
        mixed += dot(both[1024 * part : 1024 * part + 512, :], both[pl.ds(start, 256), :], NT)
    for yc in range(2):
        blocks = [mixed[128 * g : 128 * (g + 1), 128 * yc : 128 * (yc + 1)] for g in range(4)]
        for c, block in enumerate(transpose_groups(blocks)):
            scatter_block(block, stage, SUM_GROUP, ROW, {"yc": yc, **bits(("x1", "x0"), c)})
    sent[...] = stage[...].astype(BF16)


def split_kernel_in(got, left, right, stage):
    for g, block in enumerate(gather_blocks(got, IN_GROUP, ("yc", "x0"))):
        stage[...] = block
        rows = slice(128 * g, 128 * (g + 1))
        left[:, rows] = stage[pl.ds(0, 128, stride=2), :].T.astype(BF16)
        right[rows, :] = stage[pl.ds(1, 128, stride=2), :].astype(BF16)


def product_kernel_in(left, right, sent, stage, packed):
    stage[...] = dot(left[...], right[...])
    blocks = [stage[pl.ds(g, 128, stride=4), :] for g in range(4)]
    for c, block in enumerate(transpose_groups(blocks)):
        scatter_block(block, packed, IN_GROUP, ("z1", "yb", "z2", "z0", "ya"), bits(("yc", "x0"), c))
    sent[...] = packed[...].astype(BF16)


def call(kernel, outs, scratch, *operands, hbm=False):
    whole = pl.BlockSpec(memory_space=pltpu.VMEM)
    outs = [jax.ShapeDtypeStruct(shape, kind) for shape, kind in outs]
    return pl.pallas_call(
        kernel,
        out_shape=outs,
        in_specs=[pl.BlockSpec(memory_space=pltpu.HBM) if hbm else whole] * len(operands),
        out_specs=[whole] * len(outs),
        scratch_shapes=[pltpu.VMEM(s, F32) if isinstance(s, tuple) else s for s in scratch],
        compiler_params=pltpu.CompilerParams(vmem_limit_bytes=(62 if hbm else 32) * 1024 * 1024),
    )(*operands)


def exchange(values, group, size):
    got = lax.all_to_all(values.reshape(-1, size, 128), group, 0, 0, tiled=True)
    return got.reshape(values.shape)


def shards(pair, og, ob, owi, omg, omb, owo, ig, ib, iwi, img, imb, iwo):
    params = [v.reshape(1, CH) for v in (og, ob, omg, omb, ig, ib, img, imb)]
    sent, gate, pair = call(
        open_kernel,
        [((1024, 128), BF16), ((CH + 8, 512), F32), ((CH, 512), BF16)],
        [
            pltpu.VMEM(pair.shape, BF16),
            pltpu.VMEM(owi.shape, BF16),
            (1024, 128),
            pltpu.SemaphoreType.DMA((10,)),
        ],
        pair, owi, *params,
        hbm=True,
    )
    got = exchange(sent, OUT_GROUP, 8)
    (both,) = call(split_kernel_out, [((1024, 128), BF16)], [(256, 128), (512, 128)], got)
    both = lax.all_gather(both, "core", axis=0, tiled=True)
    (sent,) = call(product_kernel_out, [((1024, 128), BF16)], [(1024, 128)], both)
    got = exchange(sent, SUM_GROUP, 4)
    sent, first, gate = call(
        middle_kernel,
        [((1024, 128), BF16), ((CH, 512), BF16), ((CH + 8, 512), F32)],
        [(1024, 128), (1024, 128)],
        pair, got, gate, owo, iwi,
    )
    got = exchange(sent, IN_GROUP, 8)
    left, right = call(
        split_kernel_in,
        [((128, 512), BF16), ((512, 128), BF16)],
        [(256, 128)],
        got,
    )
    left = lax.all_gather(left, ("x1", "core"), axis=0, tiled=True)
    (sent,) = call(
        product_kernel_in, [((512, 128), BF16)], [(512, 128), (512, 128)], left, right
    )
    got = exchange(sent, IN_GROUP, 4)
    (updated,) = call(
        close_kernel,
        [((ROWS, COLS, CH), BF16)],
        [(512, 128)],
        first, got, gate, iwo,
    )
    return updated


def solution(mesh):
    fine = Mesh(mesh.devices.reshape((2,) * 9), AXES)
    return jax.shard_map(
        shards,
        mesh=fine,
        in_specs=(P(ROW, COL, None),) + (P(),) * 12,
        out_specs=P(ROW, COL, None),
        check_vma=False,
    )
```

```python
import jax
import jax.numpy as jnp
from jax import lax
from jax.experimental import pallas as pl
from jax.experimental.pallas import tpu as pltpu
from jax.sharding import Mesh, PartitionSpec as P

CH = 128
EPSILON = 1e-05
ROWS, COLS = 14, 28
F32, BF16 = jnp.float32, jnp.bfloat16

AXES = ("z2", "z1", "z0", "yb", "ya", "yc", "x1", "x0", "core")
ROW, COL = AXES[:5], AXES[5:]
OUT_GROUP = ("yb", "ya", "z0", "z1", "z2", "x1", "x0")
SUM_GROUP = OUT_GROUP + ("yc",)
IN_GROUP = ("yb", "ya", "z2", "z1", "z0", "x0", "yc")


NT = (((1,), (1,)), ((), ()))


def dot(a, b, dims=(((1,), (0,)), ((), ()))):
    return lax.dot_general(a, b, dims, preferred_element_type=F32)


def iota(shape, axis):
    return lax.broadcasted_iota(jnp.int32, shape, axis)


def residue_of_slot(slot):
    inner = slot % 16
    residue = inner % 4 * 4 + inner // 4
    return jnp.where(residue < ROWS, slot // 16 * ROWS + residue, -1)


def transpose_groups(blocks):
    lane = iota(blocks[0].shape, 1)
    low, even = lane < 64, lane // 32 % 2 == 0
    a, b, c, d = blocks
    a, c = jnp.where(low, a, pltpu.roll(c, 64, 1)), jnp.where(low, pltpu.roll(a, 64, 1), c)
    b, d = jnp.where(low, b, pltpu.roll(d, 64, 1)), jnp.where(low, pltpu.roll(b, 64, 1), d)
    a, b = jnp.where(even, a, pltpu.roll(b, 32, 1)), jnp.where(even, pltpu.roll(a, 96, 1), b)
    c, d = jnp.where(even, c, pltpu.roll(d, 32, 1)), jnp.where(even, pltpu.roll(c, 96, 1), d)
    return [a, b, c, d]


def bits(names, number):
    return {name: number >> (len(names) - 1 - n) & 1 for n, name in enumerate(names)}


def place_in(names, values):
    place = 0
    for name in names:
        place = 2 * place + values[name]
    return place


def gather_blocks(got, group, col_names):
    values = got[...].astype(F32)
    blocks = []
    for c in range(4):
        places = [place_in(group, {**bits(ROW, r), **bits(col_names, c)}) for r in range(32)]
        blocks.append(jnp.concatenate([values[8 * p : 8 * (p + 1)] for p in places], axis=0))
    return transpose_groups(blocks)


def scatter_block(block, stage, group, row_names, col_bits):
    for n in range(block.shape[0] // 4):
        place = place_in(group, {**bits(row_names, n), **col_bits})
        stage[4 * place : 4 * (place + 1), :] = block[4 * n : 4 * (n + 1)]


def layer_norm(values, gain, bias):
    center = values - jnp.mean(values, axis=0, keepdims=True)
    spread = jnp.mean(center * center, axis=0, keepdims=True)
    return center * lax.rsqrt(spread + EPSILON) * gain + bias


def columns(vectors, *rows):
    turned = vectors.T
    return [jnp.broadcast_to(turned[:, row : row + 1], (CH, 128)) for row in rows]


def project(q, values, gain, bias, weight, stage, gate):
    normed = layer_norm(values, gain, bias).astype(BF16)
    projected = dot(weight, normed)
    lane = iota((CH, 128), 1)
    valid = (lane // 32 * 4 + q < ROWS) & (residue_of_slot(lane % 32) >= 0)
    for side in range(2):
        opened = projected[2 * side * CH : (2 * side + 1) * CH]
        value = projected[(2 * side + 1) * CH : (2 * side + 2) * CH]
        operand = jnp.where(valid, jax.nn.sigmoid(opened) * value, 0.0)
        stage[pl.ds(2 * q + side, CH, stride=8), :] = operand
    gate[:CH, 128 * q : 128 * (q + 1)] = jax.nn.sigmoid(projected[4 * CH :])


def finish(q, pair, mixed, gate, gain, bias, weight):
    normed = layer_norm(mixed, gain, bias).astype(BF16)
    lanes = slice(128 * q, 128 * (q + 1))
    return (pair[:, lanes].astype(F32) + gate[:CH, lanes] * dot(weight, normed)).astype(BF16)


def open_kernel(*refs):
    pair_in, weight_in, params = refs[0], refs[1], refs[2:10]
    sent, gate, spread, pair, weight, stage, sems = refs[10:]
    pair_copy = pltpu.make_async_copy(pair_in, pair, sems.at[8])
    copies = [pltpu.make_async_copy(weight_in, weight, sems.at[9])]
    copies += [
        pltpu.make_async_copy(param, gate.at[pl.ds(CH + n, 1), pl.ds(0, CH)], sems.at[n])
        for n, param in enumerate(params)
    ]
    for copy in [pair_copy, *copies]:
        copy.start()
    pair_copy.wait()
    place = (residue_of_slot(iota((32, COLS), 0)) == iota((32, COLS), 1)).astype(BF16)
    values = []
    for q in range(4):
        parts = [
            dot(place, pair[4 * g + q]) if 4 * g + q < ROWS else jnp.zeros((32, CH), F32)
            for g in range(4)
        ]
        values.append(jnp.concatenate(parts, axis=0).T)
        spread[:, 128 * q : 128 * (q + 1)] = values[q].astype(BF16)
    for copy in copies:
        copy.wait()
    gain, bias = columns(gate[CH:, :CH], 0, 1)
    turned = weight[...].T
    for q in range(4):
        project(q, values[q], gain, bias, turned, stage, gate)
    sent[...] = stage[...].astype(BF16)


def middle_kernel(pair, got, gate, weight_out, weight, sent, first, gate_in, mixed, stage):
    mixed[...] = got[...].astype(F32)
    vectors = gate[CH:, :CH]
    gate_in[CH:, :CH] = vectors
    mix_gain, mix_bias, gain, bias = columns(vectors, 2, 3, 4, 5)
    turned_out, turned = weight_out[...].T, weight[...].T
    for q in range(4):
        values = mixed[pl.ds(q, CH, stride=8), :] + mixed[pl.ds(4 + q, CH, stride=8), :]
        values = finish(q, pair, values, gate, mix_gain, mix_bias, turned_out)
        first[:, 128 * q : 128 * (q + 1)] = values
        project(q, values.astype(F32), gain, bias, turned, stage, gate_in)
    sent[...] = stage[...].astype(BF16)


def close_kernel(first, got, gate, weight_out, updated, mixed):
    mixed[...] = got[...].astype(F32)
    gain, bias = columns(gate[CH:, :CH], 6, 7)
    turned = weight_out[...].T
    row, lane = iota((128, 128), 0), iota((128, 128), 1)
    place = (row // 32 == lane // 32) & (residue_of_slot(lane % 32) == row % 32)
    place = place.astype(F32).astype(BF16)
    for q in range(4):
        values = mixed[pl.ds(q, CH, stride=4), :]
        values = finish(q, first, values, gate, gain, bias, turned)
        values = dot(place, values, NT).astype(BF16)
        for g in range(4):
            if 4 * g + q < ROWS:
                updated[4 * g + q] = values[32 * g : 32 * g + COLS]


def split_kernel_out(got, both, stage, order):
    for g, block in enumerate(gather_blocks(got, OUT_GROUP, ("x1", "x0"))):
        stage[...] = block
        both[128 * g : 128 * (g + 1), :] = stage[pl.ds(0, 128, stride=2), :].astype(BF16)
        order[pl.ds(g, 128, stride=4), :] = stage[pl.ds(1, 128, stride=2), :]
    for c in range(16):
        target = 512 + 32 * (c % 2 * 8 + c // 2)
        both[target : target + 32, :] = order[32 * c : 32 * (c + 1), :].astype(BF16)


def product_kernel_out(both, sent, stage):
    core = lax.axis_index("core")
    mixed = jnp.zeros((512, 256), F32)
    for part in range(2):
        start = pl.multiple_of(1024 * part + 512 + 256 * core, 256)
        mixed += dot(both[1024 * part : 1024 * part + 512, :], both[pl.ds(start, 256), :], NT)
    for yc in range(2):
        blocks = [mixed[128 * g : 128 * (g + 1), 128 * yc : 128 * (yc + 1)] for g in range(4)]
        for c, block in enumerate(transpose_groups(blocks)):
            scatter_block(block, stage, SUM_GROUP, ROW, {"yc": yc, **bits(("x1", "x0"), c)})
    sent[...] = stage[...].astype(BF16)


def split_kernel_in(got, left, right, stage):
    for g, block in enumerate(gather_blocks(got, IN_GROUP, ("yc", "x0"))):
        stage[...] = block
        rows = slice(128 * g, 128 * (g + 1))
        left[:, rows] = stage[pl.ds(0, 128, stride=2), :].T.astype(BF16)
        right[rows, :] = stage[pl.ds(1, 128, stride=2), :].astype(BF16)


def product_kernel_in(left, right, sent, stage, packed):
    stage[...] = dot(left[...], right[...])
    blocks = [stage[pl.ds(g, 128, stride=4), :] for g in range(4)]
    for c, block in enumerate(transpose_groups(blocks)):
        scatter_block(block, packed, IN_GROUP, ("z1", "yb", "z2", "z0", "ya"), bits(("yc", "x0"), c))
    sent[...] = packed[...].astype(BF16)


def call(kernel, outs, scratch, *operands, hbm=False):
    whole = pl.BlockSpec(memory_space=pltpu.VMEM)
    outs = [jax.ShapeDtypeStruct(shape, kind) for shape, kind in outs]
    return pl.pallas_call(
        kernel,
        out_shape=outs,
        in_specs=[pl.BlockSpec(memory_space=pltpu.HBM) if hbm else whole] * len(operands),
        out_specs=[whole] * len(outs),
        scratch_shapes=[pltpu.VMEM(s, F32) if isinstance(s, tuple) else s for s in scratch],
        compiler_params=pltpu.CompilerParams(vmem_limit_bytes=(62 if hbm else 32) * 1024 * 1024),
    )(*operands)


def exchange(values, group, size):
    got = lax.all_to_all(values.reshape(-1, size, 128), group, 0, 0, tiled=True)
    return got.reshape(values.shape)


def shards(pair, og, ob, owi, omg, omb, owo, ig, ib, iwi, img, imb, iwo):
    params = [v.reshape(1, CH) for v in (og, ob, omg, omb, ig, ib, img, imb)]
    sent, gate, pair = call(
        open_kernel,
        [((1024, 128), BF16), ((CH + 8, 512), F32), ((CH, 512), BF16)],
        [
            pltpu.VMEM(pair.shape, BF16),
            pltpu.VMEM(owi.shape, BF16),
            (1024, 128),
            pltpu.SemaphoreType.DMA((10,)),
        ],
        pair, owi, *params,
        hbm=True,
    )
    got = exchange(sent, OUT_GROUP, 8)
    (both,) = call(split_kernel_out, [((1024, 128), BF16)], [(256, 128), (512, 128)], got)
    both = lax.all_gather(both, "core", axis=0, tiled=True)
    (sent,) = call(product_kernel_out, [((1024, 128), BF16)], [(1024, 128)], both)
    got = exchange(sent, SUM_GROUP, 4)
    sent, first, gate = call(
        middle_kernel,
        [((1024, 128), BF16), ((CH, 512), BF16), ((CH + 8, 512), F32)],
        [(1024, 128), (1024, 128)],
        pair, got, gate, owo, iwi,
    )
    got = exchange(sent, IN_GROUP, 8)
    left, right = call(
        split_kernel_in,
        [((128, 512), BF16), ((512, 128), BF16)],
        [(256, 128)],
        got,
    )
    left = lax.all_gather(left, ("x1", "core"), axis=0, tiled=True)
    (sent,) = call(
        product_kernel_in, [((512, 128), BF16)], [(512, 128), (512, 128)], left, right
    )
    got = exchange(sent, IN_GROUP, 4)
    (updated,) = call(
        close_kernel,
        [((ROWS, COLS, CH), BF16)],
        [(512, 128)],
        first, got, gate, iwo,
    )
    return updated


def solution(mesh):
    fine = Mesh(mesh.devices.reshape((2,) * 9), AXES)
    return jax.shard_map(
        shards,
        mesh=fine,
        in_specs=(P(ROW, COL, None),) + (P(),) * 12,
        out_specs=P(ROW, COL, None),
        check_vma=False,
    )
```

```python
import jax
import jax.numpy as jnp
from jax import lax
from jax.experimental import pallas as pl
from jax.experimental.pallas import tpu as pltpu
from jax.sharding import Mesh, PartitionSpec as P

CH = 128
EPSILON = 1e-05
ROWS, COLS = 14, 28
F32, BF16 = jnp.float32, jnp.bfloat16

AXES = ("z2", "z1", "z0", "yb", "ya", "yc", "x1", "x0", "core")
ROW, COL = AXES[:5], AXES[5:]
OUT_GROUP = ("yb", "ya", "z0", "z1", "z2", "x1", "x0")
SUM_GROUP = OUT_GROUP + ("yc",)
IN_GROUP = ('yb', 'ya', 'z2', 'z1', 'z0', 'yc', 'x0')


NT = (((1,), (1,)), ((), ()))


def dot(a, b, dims=(((1,), (0,)), ((), ()))):
    return lax.dot_general(a, b, dims, preferred_element_type=F32)


def iota(shape, axis):
    return lax.broadcasted_iota(jnp.int32, shape, axis)


def residue_of_slot(slot):
    inner = slot % 16
    residue = inner % 4 * 4 + inner // 4
    return jnp.where(residue < ROWS, slot // 16 * ROWS + residue, -1)


def transpose_groups(blocks):
    lane = iota(blocks[0].shape, 1)
    low, even = lane < 64, lane // 32 % 2 == 0
    a, b, c, d = blocks
    a, c = jnp.where(low, a, pltpu.roll(c, 64, 1)), jnp.where(low, pltpu.roll(a, 64, 1), c)
    b, d = jnp.where(low, b, pltpu.roll(d, 64, 1)), jnp.where(low, pltpu.roll(b, 64, 1), d)
    a, b = jnp.where(even, a, pltpu.roll(b, 32, 1)), jnp.where(even, pltpu.roll(a, 96, 1), b)
    c, d = jnp.where(even, c, pltpu.roll(d, 32, 1)), jnp.where(even, pltpu.roll(c, 96, 1), d)
    return [a, b, c, d]


def bits(names, number):
    return {name: number >> (len(names) - 1 - n) & 1 for n, name in enumerate(names)}


def place_in(names, values):
    place = 0
    for name in names:
        place = 2 * place + values[name]
    return place


def gather_blocks(got, group, col_names):
    values = got[...].astype(F32)
    blocks = []
    for c in range(4):
        places = [place_in(group, {**bits(ROW, r), **bits(col_names, c)}) for r in range(32)]
        blocks.append(jnp.concatenate([values[8 * p : 8 * (p + 1)] for p in places], axis=0))
    return transpose_groups(blocks)


def scatter_block(block, stage, group, row_names, col_bits):
    for n in range(block.shape[0] // 4):
        place = place_in(group, {**bits(row_names, n), **col_bits})
        stage[4 * place : 4 * (place + 1), :] = block[4 * n : 4 * (n + 1)]


def layer_norm(values, gain, bias):
    center = values - jnp.mean(values, axis=0, keepdims=True)
    spread = jnp.mean(center * center, axis=0, keepdims=True)
    return center * lax.rsqrt(spread + EPSILON) * gain + bias


def columns(vectors, *rows):
    turned = vectors.T
    return [jnp.broadcast_to(turned[:, row : row + 1], (CH, 128)) for row in rows]


def project(q, values, gain, bias, weight, stage, gate):
    normed = layer_norm(values, gain, bias).astype(BF16)
    projected = dot(weight, normed)
    lane = iota((CH, 128), 1)
    valid = (lane // 32 * 4 + q < ROWS) & (residue_of_slot(lane % 32) >= 0)
    for side in range(2):
        opened = projected[2 * side * CH : (2 * side + 1) * CH]
        value = projected[(2 * side + 1) * CH : (2 * side + 2) * CH]
        operand = jnp.where(valid, jax.nn.sigmoid(opened) * value, 0.0)
        stage[pl.ds(2 * q + side, CH, stride=8), :] = operand
    gate[:CH, 128 * q : 128 * (q + 1)] = jax.nn.sigmoid(projected[4 * CH :])


def finish(q, pair, mixed, gate, gain, bias, weight):
    normed = layer_norm(mixed, gain, bias).astype(BF16)
    lanes = slice(128 * q, 128 * (q + 1))
    return (pair[:, lanes].astype(F32) + gate[:CH, lanes] * dot(weight, normed)).astype(BF16)


def open_kernel(*refs):
    pair_in, weight_in, params = refs[0], refs[1], refs[2:10]
    sent, gate, spread, pair, weight, stage, sems = refs[10:]
    pair_copy = pltpu.make_async_copy(pair_in, pair, sems.at[8])
    copies = [pltpu.make_async_copy(weight_in, weight, sems.at[9])]
    copies += [
        pltpu.make_async_copy(param, gate.at[pl.ds(CH + n, 1), pl.ds(0, CH)], sems.at[n])
        for n, param in enumerate(params)
    ]
    for copy in [pair_copy, *copies]:
        copy.start()
    pair_copy.wait()
    place = (residue_of_slot(iota((32, COLS), 0)) == iota((32, COLS), 1)).astype(BF16)
    values = []
    for q in range(4):
        parts = [
            dot(place, pair[4 * g + q]) if 4 * g + q < ROWS else jnp.zeros((32, CH), F32)
            for g in range(4)
        ]
        values.append(jnp.concatenate(parts, axis=0).T)
        spread[:, 128 * q : 128 * (q + 1)] = values[q].astype(BF16)
    for copy in copies:
        copy.wait()
    gain, bias = columns(gate[CH:, :CH], 0, 1)
    turned = weight[...].T
    for q in range(4):
        project(q, values[q], gain, bias, turned, stage, gate)
    sent[...] = stage[...].astype(BF16)


def middle_kernel(pair, got, gate, weight_out, weight, sent, first, gate_in, mixed, stage):
    mixed[...] = got[...].astype(F32)
    vectors = gate[CH:, :CH]
    gate_in[CH:, :CH] = vectors
    mix_gain, mix_bias, gain, bias = columns(vectors, 2, 3, 4, 5)
    turned_out, turned = weight_out[...].T, weight[...].T
    for q in range(4):
        values = mixed[pl.ds(q, CH, stride=8), :] + mixed[pl.ds(4 + q, CH, stride=8), :]
        values = finish(q, pair, values, gate, mix_gain, mix_bias, turned_out)
        first[:, 128 * q : 128 * (q + 1)] = values
        project(q, values.astype(F32), gain, bias, turned, stage, gate_in)
    sent[...] = stage[...].astype(BF16)


def close_kernel(first, got, gate, weight_out, updated, mixed):
    mixed[...] = got[...].astype(F32)
    gain, bias = columns(gate[CH:, :CH], 6, 7)
    turned = weight_out[...].T
    row, lane = iota((128, 128), 0), iota((128, 128), 1)
    place = (row // 32 == lane // 32) & (residue_of_slot(lane % 32) == row % 32)
    place = place.astype(F32).astype(BF16)
    for q in range(4):
        values = mixed[pl.ds(q, CH, stride=4), :]
        values = finish(q, first, values, gate, gain, bias, turned)
        values = dot(place, values, NT).astype(BF16)
        for g in range(4):
            if 4 * g + q < ROWS:
                updated[4 * g + q] = values[32 * g : 32 * g + COLS]


def split_kernel_out(got, both, stage, order):
    for g, block in enumerate(gather_blocks(got, OUT_GROUP, ("x1", "x0"))):
        stage[...] = block
        both[128 * g : 128 * (g + 1), :] = stage[pl.ds(0, 128, stride=2), :].astype(BF16)
        order[pl.ds(g, 128, stride=4), :] = stage[pl.ds(1, 128, stride=2), :]
    for c in range(16):
        target = 512 + 32 * (c % 2 * 8 + c // 2)
        both[target : target + 32, :] = order[32 * c : 32 * (c + 1), :].astype(BF16)


def product_kernel_out(both, sent, stage):
    core = lax.axis_index("core")
    mixed = jnp.zeros((512, 256), F32)
    for part in range(2):
        start = pl.multiple_of(1024 * part + 512 + 256 * core, 256)
        mixed += dot(both[1024 * part : 1024 * part + 512, :], both[pl.ds(start, 256), :], NT)
    for yc in range(2):
        blocks = [mixed[128 * g : 128 * (g + 1), 128 * yc : 128 * (yc + 1)] for g in range(4)]
        for c, block in enumerate(transpose_groups(blocks)):
            scatter_block(block, stage, SUM_GROUP, ROW, {"yc": yc, **bits(("x1", "x0"), c)})
    sent[...] = stage[...].astype(BF16)


def split_kernel_in(got, left, right, stage):
    for g, block in enumerate(gather_blocks(got, IN_GROUP, ("yc", "x0"))):
        stage[...] = block
        rows = slice(128 * g, 128 * (g + 1))
        left[:, rows] = stage[pl.ds(0, 128, stride=2), :].T.astype(BF16)
        right[rows, :] = stage[pl.ds(1, 128, stride=2), :].astype(BF16)


def product_kernel_in(left, right, sent, stage, packed):
    stage[...] = dot(left[...], right[...])
    blocks = [stage[pl.ds(g, 128, stride=4), :] for g in range(4)]
    for c, block in enumerate(transpose_groups(blocks)):
        scatter_block(block, packed, IN_GROUP, ("yb", "z1", "z2", "z0", "ya"), bits(("yc", "x0"), c))
    sent[...] = packed[...].astype(BF16)


def call(kernel, outs, scratch, *operands, hbm=False):
    whole = pl.BlockSpec(memory_space=pltpu.VMEM)
    outs = [jax.ShapeDtypeStruct(shape, kind) for shape, kind in outs]
    return pl.pallas_call(
        kernel,
        out_shape=outs,
        in_specs=[pl.BlockSpec(memory_space=pltpu.HBM) if hbm else whole] * len(operands),
        out_specs=[whole] * len(outs),
        scratch_shapes=[pltpu.VMEM(s, F32) if isinstance(s, tuple) else s for s in scratch],
        compiler_params=pltpu.CompilerParams(vmem_limit_bytes=(62 if hbm else 32) * 1024 * 1024),
    )(*operands)


def exchange(values, group, size):
    got = lax.all_to_all(values.reshape(-1, size, 128), group, 0, 0, tiled=True)
    return got.reshape(values.shape)


def shards(pair, og, ob, owi, omg, omb, owo, ig, ib, iwi, img, imb, iwo):
    params = [v.reshape(1, CH) for v in (og, ob, omg, omb, ig, ib, img, imb)]
    sent, gate, pair = call(
        open_kernel,
        [((1024, 128), BF16), ((CH + 8, 512), F32), ((CH, 512), BF16)],
        [
            pltpu.VMEM(pair.shape, BF16),
            pltpu.VMEM(owi.shape, BF16),
            (1024, 128),
            pltpu.SemaphoreType.DMA((10,)),
        ],
        pair, owi, *params,
        hbm=True,
    )
    got = exchange(sent, OUT_GROUP, 8)
    (both,) = call(split_kernel_out, [((1024, 128), BF16)], [(256, 128), (512, 128)], got)
    both = lax.all_gather(both, "core", axis=0, tiled=True)
    (sent,) = call(product_kernel_out, [((1024, 128), BF16)], [(1024, 128)], both)
    got = exchange(sent, SUM_GROUP, 4)
    sent, first, gate = call(
        middle_kernel,
        [((1024, 128), BF16), ((CH, 512), BF16), ((CH + 8, 512), F32)],
        [(1024, 128), (1024, 128)],
        pair, got, gate, owo, iwi,
    )
    got = exchange(sent, IN_GROUP, 8)
    left, right = call(
        split_kernel_in,
        [((128, 512), BF16), ((512, 128), BF16)],
        [(256, 128)],
        got,
    )
    left = lax.all_gather(left, ("core", "x1"), axis=0, tiled=True)
    (sent,) = call(
        product_kernel_in, [((512, 128), BF16)], [(512, 128), (512, 128)], left, right
    )
    got = exchange(sent, IN_GROUP, 4)
    (updated,) = call(
        close_kernel,
        [((ROWS, COLS, CH), BF16)],
        [(512, 128)],
        first, got, gate, iwo,
    )
    return updated


def solution(mesh):
    fine = Mesh(mesh.devices.reshape((2,) * 9), AXES)
    return jax.shard_map(
        shards,
        mesh=fine,
        in_specs=(P(ROW, COL, None),) + (P(),) * 12,
        out_specs=P(ROW, COL, None),
        check_vma=False,
    )
```
